128 devices in a mesh: dp: 32 (over y, x_hi, z), tensor: 4 (over x_lo, core).
Axes of the slice: x: 4 (x_hi: 2, x_lo: 2; x = x_hi * 2 + x_lo), y: 4, z: 4, core: 2. Of those that a mesh axis runs over, the one named last changes fastest.
Arguments:
- tokens: bfloat16 [12288, 2048], P('dp'), may hold values from -6 to 6
- seq_lengths: int32 [128], P('dp'), may hold values from 0 to 384, as said below
- attention_gain: float32 [2048], replicated, may hold values from 0.1 to 1.9
- feedforward_gain: float32 [2048], replicated, may hold values from 0.1 to 1.9
- query_weight: bfloat16 [2048, 2048], P('dp', 'tensor'), may hold values from -0.125 to 0.125
- key_weight: bfloat16 [2048, 2048], P('dp', 'tensor'), may hold values from -0.125 to 0.125
- value_weight: bfloat16 [2048, 2048], P('dp', 'tensor'), may hold values from -0.125 to 0.125
- output_weight: bfloat16 [2048, 2048], P('tensor', 'dp'), may hold values from -0.75 to 0.75
- gate_weight: bfloat16 [2048, 8192], P('dp', 'tensor'), may hold values from -0.125 to 0.125
- up_weight: bfloat16 [2048, 8192], P('dp', 'tensor'), may hold values from -0.125 to 0.125
- down_weight: bfloat16 [8192, 2048], P('tensor', 'dp'), may hold values from -0.0625 to 0.0625
- cotangent: bfloat16 [12288, 2048], P('dp'), may hold values from -6 to 6
Outputs:
- layer_out: bfloat16 [12288, 2048], P('dp')
- tokens_grad: float32 [12288, 2048], P('dp')
- attention_gain_grad: float32 [2048], replicated
- feedforward_gain_grad: float32 [2048], replicated
- query_grad: float32 [2048, 2048], P('dp', 'tensor')
- key_grad: float32 [2048, 2048], P('dp', 'tensor')
- value_grad: float32 [2048, 2048], P('dp', 'tensor')
- output_grad: float32 [2048, 2048], P('tensor', 'dp')
- gate_grad: float32 [2048, 8192], P('dp', 'tensor')
- up_grad: float32 [2048, 8192], P('dp', 'tensor')
- down_grad: float32 [8192, 2048], P('tensor', 'dp')
The draws below stay inside these ranges and needn't reach their ends.
Inputs may be any that keep to these rules, and one draw needn't show every extreme that they name: `seq_lengths`: each device's 4 lengths sum to between 192 and 384; lengths may be 0; in every draw some device holds a single sequence of 384 rows.
All inputs are finite; a program needn't handle non-finite values.
Results may differ from the reference program's by a relative error of at most 0.025.
Values may be sent and summed in bfloat16 or wider, within the bound.
No kernel may reach another device: no remote copies, remote signals or barrier semaphores. Data moves between devices by JAX's collectives and lax.ppermute only.
A program may use at most 192 MiB of HBM per device.

```python
import jax
import jax.numpy as jnp
from jax import lax

D = 2048
HEADS = 32
HEAD = 64
FF = 8192
TOK_DEV = 384
SEQS_DEV = 4
HD = 2048
TOKENS = 12288
N_DP = 32


def draw_seq_lengths(key, part):
    key = jax.random.fold_in(key, 11)
    key_total, key_cuts, key_full = jax.random.split(key, 3)
    totals = jax.random.randint(key_total, (N_DP,), TOK_DEV // 2, TOK_DEV + 1).astype(jnp.int32)
    cuts = jax.random.randint(key_cuts, (N_DP, SEQS_DEV - 1), 0, TOK_DEV + 1).astype(jnp.int32)
    cuts = jnp.minimum(cuts, totals[:, None])
    cuts = jnp.sort(cuts, axis=1)
    chosen = jax.random.randint(key_full, (), 0, N_DP)
    is_full = jnp.arange(N_DP) == chosen
    totals = jnp.where(is_full, TOK_DEV, totals)
    cuts = jnp.where(is_full[:, None], TOK_DEV, cuts)
    edges = jnp.concatenate([jnp.zeros((N_DP, 1), jnp.int32), cuts, totals[:, None]], axis=1)
    lengths = edges[:, 1:] - edges[:, :-1]
    return lengths.reshape(-1).astype(jnp.int32)


def raised(values, stream_key, source, target, blocks, factor):
    def block_of(dim):
        return (jnp.arange(values.shape[dim]) // (values.shape[dim] // blocks)).reshape((-1,) + (1,) * (values.ndim - 1 - dim))

    near = jax.random.permutation(stream_key, blocks)[block_of(target)]
    other_side = (block_of(target) + blocks // 2) % blocks
    return jnp.where((block_of(source) == near) | (block_of(source) == other_side), factor * values, values)


def levels(rng, shape, pieces, low, largest):
    level, own = 1.0, jax.random.fold_in(rng, 6)
    for dim, shards_of in pieces:
        heights = jnp.exp(jax.random.uniform(jax.random.fold_in(own, dim), (shards_of,), jnp.float32, low / len(pieces), largest / len(pieces)))
        level = level * jnp.repeat(heights, shape[dim] // shards_of).reshape([-1 if axis == dim else 1 for axis in range(len(shape))])
    return level


def bell_draw(rng, shape, width, bound, shards=(), kind=jnp.bfloat16):
    entries = jax.random.normal(rng, shape, jnp.float32) * width
    if len(shards) > 0:
        entries = levels(rng, shape, shards, -0.22, 0.18) * entries
    return jnp.clip(entries, min=-bound, max=bound).astype(kind)


def gaussian_with(rng, dims, spread, bound, shards, heavy, kind=jnp.bfloat16):
    drawn = spread * jax.random.normal(rng, dims, jnp.float32)
    if shards:
        drawn = drawn * levels(rng, dims, shards, -0.22, 0.18)
    return jnp.clip(raised(drawn, jax.random.fold_in(rng, 3), *heavy), -bound, bound).astype(kind)


def setup_inputs(seed: int = 0) -> dict:
    splits = jax.random.split(jax.random.key(seed), 13)
    return {
        "tokens": gaussian_with(splits[0], (TOKENS, D), 1.0, 6.0, ((0, 32),), (0, 1, 32, 2.75)),
        "seq_lengths": draw_seq_lengths(jax.random.fold_in(splits[12], 71), 0),
        "attention_gain": jnp.clip(1.0 + 0.18 * jax.random.normal(splits[2], (D,), jnp.float32), 0.1, 1.9),
        "feedforward_gain": jnp.clip(1.0 + 0.18 * jax.random.normal(splits[3], (D,), jnp.float32), 0.1, 1.9),
        "query_weight": bell_draw(splits[4], (D, HD), D ** -0.5, 0.125, ((0, 32), (1, 4))),
        "key_weight": bell_draw(splits[5], (D, HD), D ** -0.5, 0.125, ((0, 32), (1, 4))),
        "value_weight": bell_draw(splits[6], (D, HD), D ** -0.5, 0.125, ((0, 32), (1, 4))),
        "output_weight": bell_draw(splits[7], (HD, D), (HD // 32) ** -0.5, 0.75, ((0, 4), (1, 32))),
        "gate_weight": bell_draw(splits[8], (D, FF), D ** -0.5, 0.125, ((0, 32), (1, 4))),
        "up_weight": bell_draw(splits[9], (D, FF), D ** -0.5, 0.125, ((0, 32), (1, 4))),
        "down_weight": bell_draw(splits[10], (FF, D), FF ** -0.5, 0.0625, ((0, 4), (1, 32))),
        "cotangent": gaussian_with(splits[11], (TOKENS, D), 1.0, 6.0, ((0, 32),), (0, 1, 32, 2.75)),
    }


@jax.custom_vjp
def low(v):
    return lax.optimization_barrier(v.astype(jnp.bfloat16)).astype(jnp.float32)

@jax.custom_vjp
def low_back(v):
    return v

def low_keep(v):
    return (low(v), None)

def low_pass(kept, grad):
    return (grad,)

def back_keep(v):
    return (v, None)

def back_low(kept, grad):
    return (low(grad),)
low.defvjp(low_keep, low_pass)
low_back.defvjp(back_keep, back_low)
norm_epsilon = 1e-05
rope_base = 130000.0

def product(left, right):
    return jnp.dot(left, right, precision=lax.Precision.HIGHEST, preferred_element_type=jnp.float32)

def layout(lengths):
    ends = jnp.cumsum(lengths).astype(jnp.int32)
    places = jnp.arange(TOK_DEV, dtype=jnp.int32)
    passed = places[:, None] >= ends[None, :]
    segment = lax.optimization_barrier(jnp.sum(passed.astype(jnp.int32), axis=1)).astype(jnp.int32)
    begins = lax.optimization_barrier(jnp.max(jnp.where(passed, ends[None, :], jnp.zeros_like(ends)[None, :]), axis=1))
    return (segment, (places - begins).astype(jnp.int32))

def rotary(position):
    index = jnp.arange(HEAD // 2, dtype=jnp.float32)
    frequency = rope_base ** (-2.0 * index / HEAD)
    angle = position.astype(jnp.float32)[:, None] * frequency[None, :]
    return (jnp.cos(angle)[:, None, :], jnp.sin(angle)[:, None, :])

def rotate(values, cosine, sine):
    half = values.shape[-1] // 2
    first, second = (values[..., :half], values[..., half:])
    return jnp.concatenate([first * cosine - second * sine, second * cosine + first * sine], axis=-1)

def normalize(values, gain):
    scale = lax.rsqrt(lax.optimization_barrier(jnp.mean(values * values, axis=-1, keepdims=True)) + norm_epsilon)
    return values * scale * gain

def attend(query_block, key_block, value_block, segment):
    scores = jnp.einsum('qhd,khd->hqk', query_block, key_block, precision=lax.Precision.HIGHEST)
    scores = low_back(scores)
    places = jnp.arange(segment.shape[0], dtype=jnp.int32)
    allowed = (segment[:, None] == segment[None, :]) & (places[:, None] >= places[None, :])
    scores = jnp.where(allowed[None], scores, -1000000000.0)
    weights = jax.nn.softmax(scores, axis=-1)
    return jnp.einsum('hqk,khd->qhd', low(weights), value_block, precision=lax.Precision.HIGHEST)

def attend_parts(parts):
    return jax.checkpoint(attend)(*parts)

def forward(hidden, segment, position, gain_one, gain_two, query_weight, key_weight, value_weight, output_weight, gate_weight, up_weight, down_weight):
    rows = hidden.shape[0]
    normed = low(normalize(hidden, gain_one))
    cosine, sine = rotary(position)
    query = low_back(product(normed, query_weight)).reshape(rows, HEADS, HEAD)
    query = low(rotate(query, cosine, sine) * HEAD ** (-0.5))
    key_rot = low_back(product(normed, key_weight)).reshape(rows, HEADS, HEAD)
    key_rot = low(rotate(key_rot, cosine, sine))
    value_low = low(low_back(product(normed, value_weight))).reshape(rows, HEADS, HEAD)

    def blocks(array):
        return array.reshape((N_DP, TOK_DEV) + array.shape[1:])
    attended = lax.map(attend_parts, (blocks(query), blocks(key_rot), blocks(value_low), blocks(segment)))
    attended = low(low_back(attended.reshape(rows, HD)))
    branch = low_back(product(attended, output_weight))
    middle = hidden + branch
    normed_two = low(normalize(middle, gain_two))
    gate_value = low_back(product(normed_two, gate_weight))
    up_value = low_back(product(normed_two, up_weight))
    mixed = low(jax.nn.silu(gate_value) * up_value)
    return middle + low_back(product(mixed, down_weight))

def reference(tokens, seq_lengths, attention_gain, feedforward_gain, query_weight, key_weight, value_weight, output_weight, gate_weight, up_weight, down_weight, cotangent):
    segment, position = jax.vmap(layout)(seq_lengths.reshape(N_DP, SEQS_DEV))
    segment = segment.reshape(-1)
    position = position.reshape(-1)
    floats = [tokens, attention_gain, feedforward_gain, query_weight, key_weight, value_weight, output_weight, gate_weight, up_weight, down_weight]
    floats = [array.astype(jnp.float32) for array in floats]

    def wrapped(hidden, gain_one, gain_two, wq_full, wk_full, wv_full, wo_full, wg_full, wu_full, wd_full):
        return forward(hidden, segment, position, gain_one, gain_two, wq_full, wk_full, wv_full, wo_full, wg_full, wu_full, wd_full)
    result, pullback = jax.vjp(wrapped, *floats)
    grads = pullback(cotangent.astype(jnp.float32))
    return (result.astype(jnp.bfloat16), grads[0], grads[1], grads[2], grads[3], grads[4], grads[5], grads[6], grads[7], grads[8], grads[9])
```

```python
import functools

import jax
import jax.numpy as jnp
from jax import lax
from jax.experimental import pallas as pl
from jax.experimental.pallas import tpu as pltpu
from jax.sharding import Mesh, PartitionSpec as P

HEAD = 64
MIB = 1024 * 1024

norm_epsilon = 1e-05
rope_base = 130000.0
masked_score = -1000000000.0

AXES = ("y", "xh", "z", "xl", "c")
SIZES = (4, 2, 4, 2, 2)
DP = ("y", "xh", "z")
TP = ("xl", "c")

f32 = jnp.float32
bf16 = jnp.bfloat16


def swap(axis, mask, size):
    perm = [(i, i ^ mask) for i in range(size)]
    return lambda value: lax.ppermute(value, axis, perm)


core = swap("c", 1, 2)
y_ring = (swap("y", 1, 4), swap("y", 3, 4), swap("y", 2, 4))
z_ring = (swap("z", 1, 4), swap("z", 3, 4), swap("z", 2, 4))
x_ring = (swap(("xh", "xl"), 1, 4), swap(("xh", "xl"), 3, 4), swap(("xh", "xl"), 2, 4))


def ring_first(parts, ring):
    return ring[0](parts[2]), ring[1](parts[3])


def ring_between(parts, arrived):
    half = parts[2].shape[0]
    to_third, to_first = arrived
    first = jnp.concatenate([parts[1][:half], parts[1][half:] + to_first], axis=0)
    third = jnp.concatenate([parts[4][:half] + to_third, parts[4][half:]], axis=0)
    return first, third


def both_ways(values, ring):
    return ring[0](values[0]), ring[1](values[1])


def line_gather(own):
    sides = both_ways((own, own), x_ring)
    mine = stacked(ring_pieces(own, sides, opposite_halves(sides, x_ring)))
    return stacked([mine, core(mine)])


def opposite_halves(arrived, ring):
    first, third = arrived
    half = first.shape[0] // 2
    return ring[0](third[:half]), ring[1](first[half:])


def ring_pieces(own, arrived, halves):
    return [own, arrived[0], *halves, arrived[1]]


def direct(value, ring):
    near, far, opposite = ring
    return near(value), opposite(value), far(value)


def sum_round(value, arrived):
    near, opposite, far = arrived
    return (value + near) + (opposite + far)


def total(terms):
    result = terms[0].astype(f32)
    for term in terms[1:]:
        result = result + term.astype(f32)
    return result


def sum_split_kernel(terms, *refs):
    row = 0
    for out in refs[terms:]:
        rows = out.shape[0]
        value = refs[0][row : row + rows, :].astype(f32)
        for ref in refs[1:terms]:
            value = value + ref[row : row + rows, :].astype(f32)
        out[...] = value.astype(out.dtype)
        row += rows


def sum_split(terms, cuts):
    width = terms[0].shape[1]
    whole = pl.BlockSpec(memory_space=pltpu.VMEM)
    rows = sum(cuts)
    return pl.pallas_call(
        functools.partial(sum_split_kernel, len(terms)),
        out_shape=[jax.ShapeDtypeStruct((cut, width), bf16) for cut in cuts],
        in_specs=[whole] * len(terms),
        out_specs=[whole] * len(cuts),
        cost_estimate=pl.CostEstimate(
            flops=rows * width * len(terms),
            bytes_accessed=rows * width * 2 * (len(terms) + 1),
            transcendentals=0,
        ),
        compiler_params=pltpu.CompilerParams(vmem_limit_bytes=2 * rows * width * 2 * (len(terms) + 1) + 4 * MIB),
        name="sum_split",
    )(*terms)


def ring_cuts(rows):
    quarter = rows // 4
    return (quarter, quarter, quarter // 2, quarter // 2, quarter)


def pack_kernel(moves, count, offsets, *refs):
    sems = refs[-1]

    def at(row):
        return row if isinstance(row, int) else pl.multiple_of(offsets[row[0]], 16)

    copies = []
    for k, (i, start, rows, out, to, column, columns) in enumerate(moves):
        copies.append(
            pltpu.make_async_copy(
                refs[i].at[pl.ds(at(start), rows), pl.ds(column, columns)],
                refs[count + out].at[pl.ds(at(to), rows), :],
                sems.at[k],
            )
        )
    for copy in copies:
        copy.start()
    for copy in copies:
        copy.wait()


def pack(pieces, moves, offsets, shapes):
    anywhere = pl.BlockSpec(memory_space=pl.ANY)
    total = 2 * sum(2 * r * c for r, c in shapes)
    return pl.pallas_call(
        functools.partial(pack_kernel, tuple(moves), len(pieces)),
        out_shape=[jax.ShapeDtypeStruct(shape, pieces[0].dtype) for shape in shapes],
        in_specs=[pl.BlockSpec(memory_space=pltpu.SMEM)] + [anywhere] * len(pieces),
        out_specs=[pl.BlockSpec(memory_space=pltpu.VMEM)] * len(shapes),
        scratch_shapes=[pltpu.SemaphoreType.DMA((len(moves),))],
        compiler_params=pltpu.CompilerParams(vmem_limit_bytes=total + 2 * MIB),
        cost_estimate=pl.CostEstimate(flops=0, bytes_accessed=total, transcendentals=0),
        name="pack",
    )(offsets, *pieces)


def stacked(pieces):
    moves, row = [], 0
    for i, p in enumerate(pieces):
        moves.append((i, 0, p.shape[0], 0, row, 0, p.shape[1]))
        row += p.shape[0]
    offsets = jnp.zeros((1,), jnp.int32)
    return pack(pieces, moves, offsets, [(row, pieces[0].shape[1])])[0]


def choose_kernel(moves, count, *refs):
    sems = refs[-1]
    xh = lax.axis_index("xh")
    which = (xh, 1 - xh)
    copies = []
    for k, (i, half, start, width, to) in enumerate(moves):
        for out in range(2):
            at = pl.multiple_of(which[out] * half + start, 128)
            copies.append(
                pltpu.make_async_copy(
                    refs[i].at[:, pl.ds(at, width)],
                    refs[count + out].at[:, pl.ds(to, width)],
                    sems.at[2 * k + out],
                )
            )
    for copy in copies:
        copy.start()
    for copy in copies:
        copy.wait()


def own_columns(blocks, tiles):
    moves, to = [], 0
    for k, start, width in tiles:
        moves.append((k, blocks[k].shape[1] // 2, start, width, to))
        to += width
    rows = blocks[0].shape[0]
    anywhere = pl.BlockSpec(memory_space=pl.ANY)
    return pl.pallas_call(
        functools.partial(choose_kernel, tuple(moves), len(blocks)),
        out_shape=[jax.ShapeDtypeStruct((rows, to), bf16)] * 2,
        in_specs=[anywhere] * len(blocks),
        out_specs=[pl.BlockSpec(memory_space=pltpu.VMEM)] * 2,
        scratch_shapes=[pltpu.SemaphoreType.DMA((2 * len(moves),))],
        compiler_params=pltpu.CompilerParams(vmem_limit_bytes=56 * MIB),
        cost_estimate=pl.CostEstimate(flops=0, bytes_accessed=8 * rows * to, transcendentals=0),
        name="choose",
    )(*blocks)


def gather_weights(sent, xh):
    own = jnp.concatenate(to_columns(*both_ways(sent, x_ring), xh), axis=0)
    return lax.all_gather(own, ("y", "z"), axis=0, tiled=True)


def to_columns(first, second, xh):
    return jnp.where(xh == 0, first, second), jnp.where(xh == 0, second, first)


def deliver_kernel(moves, which, same_ref, other_ref, *outs):
    mine = which[0] == 0
    for out, start, width, at in moves:
        same, other = same_ref[:, start : start + width], other_ref[:, start : start + width]
        half = outs[out].shape[1] // 2
        outs[out][:, at : at + width] = jnp.where(mine, same, other).astype(f32)
        outs[out][:, half + at : half + at + width] = jnp.where(mine, other, same).astype(f32)


def delivered(same, other, xh, tiles, widths):
    moves, start = [], 0
    for out, at, width in tiles:
        moves.append((out, start, width, at))
        start += width
    whole = pl.BlockSpec(memory_space=pltpu.VMEM)
    rows = same.shape[0]
    return pl.pallas_call(
        functools.partial(deliver_kernel, tuple(moves)),
        out_shape=[jax.ShapeDtypeStruct((rows, width), f32) for width in widths],
        in_specs=[pl.BlockSpec(memory_space=pltpu.SMEM), whole, whole],
        out_specs=[whole] * len(widths),
        cost_estimate=pl.CostEstimate(
            flops=0, bytes_accessed=12 * rows * start, transcendentals=0
        ),
        compiler_params=pltpu.CompilerParams(vmem_limit_bytes=12 * MIB),
        name="delivered",
    )(jnp.stack([xh]).astype(jnp.int32), same, other)


def by_tensor(pieces, moves, rows, xl, c, count=1):
    width = pieces[0].shape[1] // count
    offsets = jnp.stack([((xl ^ m[2]) * 2 + (c ^ m[3])) * rows for m in moves]).astype(jnp.int32)
    moves = [
        (m[0], m[1], rows, out, (k,), out * width, width)
        for k, m in enumerate(moves)
        for out in range(count)
    ]
    return pack(pieces, moves, offsets, [(4 * rows, width)] * count)


def line_offsets(rows, xl, c):
    places = [((xl ^ r_xl) * 2 + (c ^ r_c)) * rows for r_c in range(2) for r_xl in range(2)]
    return jnp.stack(places).astype(jnp.int32)


def for_the_line(value, rows, offsets):
    width = value.shape[1]
    moves = [(0, (1 - k,), rows, 0, k * rows, 0, width) for k in range(2)]
    return pack([value], moves, offsets, [(2 * rows, width)])[0]


def of_the_line(value, other, rows, offsets):
    width = value.shape[1]
    moves = []
    for r_c in range(2):
        to = 4 * r_c * rows
        moves += [(0, (2 * r_c + k,), rows, 0, to + k * rows, 0, width) for k in range(2)]
        moves.append((1 + r_c, 0, 2 * rows, 0, to + 2 * rows, 0, width))
    return pack([value, other, core(other)], moves, offsets, [(8 * rows, width)])[0]


def layout(lengths, places):
    ends = jnp.cumsum(lengths)
    passed = places[:, None] >= ends[None, :]
    segment = jnp.sum(passed.astype(jnp.int32), axis=1)
    begins = jnp.max(jnp.where(passed, ends[None, :], jnp.zeros_like(ends)[None, :]), axis=1)
    return (segment, places - begins)


def rotary(position):
    lane = jnp.arange(2 * HEAD, dtype=jnp.int32)
    index = (lane % (HEAD // 2)).astype(f32)
    frequency = rope_base ** (-2.0 * index / HEAD)
    angle = position.astype(f32)[:, None] * frequency[None, :]
    sign = jnp.where(lane % HEAD < HEAD // 2, -1.0, 1.0).astype(f32)
    return (jnp.cos(angle), jnp.sin(angle) * sign[None, :])


def other_half(values):
    width = values.shape[1]
    half = HEAD // 2
    lane = lax.broadcasted_iota(jnp.int32, values.shape, 1)
    up, down = pltpu.roll(values, width - half, 1), pltpu.roll(values, half, 1)
    return jnp.where(lane % HEAD < half, up, down)


def widened(table, width):
    return jnp.concatenate([table] * (width // table.shape[1]), axis=1)


def attend_kernel(qkv_ref, cos_ref, sin_ref, mask_ref, rot_ref, out_ref, lse_ref):
    _, _, part, width = qkv_ref.shape
    rows, width = 2 * part, width // 3

    def columns(ref, start, size):
        return ref[:, :, :, start : start + size].reshape(rows, size)

    cosine = widened(columns(cos_ref, 0, cos_ref.shape[3]), width)
    sine = widened(columns(sin_ref, 0, sin_ref.shape[3]), width)
    query = columns(qkv_ref, 0, width)
    query = ((query * cosine + other_half(query) * sine) * HEAD ** (-0.5)).astype(bf16)
    key = columns(qkv_ref, width, width)
    key = (key * cosine + other_half(key) * sine).astype(bf16)
    value = columns(qkv_ref, 2 * width, width).astype(bf16)
    for i, low in enumerate((query, key, value)):
        rot_ref[:, :, :, i * width : (i + 1) * width] = low.reshape(2, 1, part, width)
    value_t = value.astype(f32).T.astype(bf16)
    allowed = mask_ref[0] > 0.0
    lane = lax.broadcasted_iota(jnp.int32, query.shape, 1) // HEAD
    outs = []
    for head in range(width // HEAD):
        one = jnp.where(lane == head, query, jnp.zeros_like(query))
        scores = jnp.where(allowed, dot_right_t(key, one), masked_score)
        top = jnp.max(scores, axis=0, keepdims=True)
        total = top + jnp.log(jnp.sum(jnp.exp(scores - top), axis=0, keepdims=True))
        probs = jnp.exp(scores - total).astype(bf16)
        lse_ref[0, head : head + 1, :] = total
        outs.append(local_dot(value_t[head * HEAD : (head + 1) * HEAD], probs))
    out = jnp.concatenate(outs, axis=0).T
    out_ref[...] = out.astype(bf16).reshape(2, 1, part, width)


def attend_back_kernel(
    rot_ref, grad_ref, lse_ref, cos_ref, sin_ref, mask_ref, out_ref, dv_ref, dk_ref, dq_ref
):
    _, _, part, width = grad_ref.shape
    rows = 2 * part

    def columns(ref, start, size):
        return ref[:, :, :, start : start + size].reshape(rows, size)

    query, key, value = (columns(rot_ref, i * width, width) for i in range(3))
    grad = columns(grad_ref, 0, width)
    key_t = key.astype(f32).T.astype(bf16)
    allowed = mask_ref[0] > 0.0
    lane = lax.broadcasted_iota(jnp.int32, query.shape, 1) // HEAD
    for head in range(width // HEAD):
        one = jnp.where(lane == head, query, jnp.zeros_like(query))
        one_grad = jnp.where(lane == head, grad, jnp.zeros_like(grad))
        scores = jnp.where(allowed, dot_right_t(key, one), masked_score)
        probs = jnp.exp(scores - lse_ref[0, head : head + 1, :])
        prob_grad = dot_right_t(value, one_grad)
        shift = jnp.sum(probs * prob_grad, axis=0, keepdims=True)
        score_grad = (probs * (prob_grad - shift)).astype(bf16)
        dv = local_dot(probs.astype(bf16), one_grad)
        dk = local_dot(score_grad, one)
        if head == 0:
            dv_ref[...] = dv
            dk_ref[...] = dk
        else:
            dv_ref[...] += dv
            dk_ref[...] += dk
        dq_ref[head * HEAD : (head + 1) * HEAD, :] = local_dot(
            key_t[head * HEAD : (head + 1) * HEAD], score_grad
        )
    cosine = widened(columns(cos_ref, 0, cos_ref.shape[3]), width)
    sine = widened(columns(sin_ref, 0, sin_ref.shape[3]), width)
    dq = dq_ref[...].T * HEAD ** (-0.5)
    dq = dq * cosine - other_half(dq) * sine
    dk = dk_ref[...]
    dk = dk * cosine - other_half(dk) * sine
    for i, term in enumerate((dq, dk, dv_ref[...])):
        out_ref[:, :, :, i * width : (i + 1) * width] = term.astype(bf16).reshape(
            2, 1, part, width
        )


def by_block(columns, part):
    return pl.BlockSpec((2, 1, part, columns), lambda i: (0, i, 0, 0))


def attend(qkv, cosine, sine, mask):
    rows, width = qkv.shape
    part, width = rows // 4, width // 3
    heads = width // HEAD
    table = cosine.shape[1]
    rot, out, lse = pl.pallas_call(
        attend_kernel,
        grid=(2,),
        in_specs=[
            by_block(3 * width, part),
            by_block(table, part),
            by_block(table, part),
            pl.BlockSpec((1, 2 * part, 2 * part), lambda i: (i, 0, 0)),
        ],
        out_specs=[
            by_block(3 * width, part),
            by_block(width, part),
            pl.BlockSpec((1, heads, 2 * part), lambda i: (i, 0, 0)),
        ],
        out_shape=[
            jax.ShapeDtypeStruct((2, 2, part, 3 * width), bf16),
            jax.ShapeDtypeStruct((2, 2, part, width), bf16),
            jax.ShapeDtypeStruct((2, heads, 2 * part), f32),
        ],
        cost_estimate=pl.CostEstimate(
            flops=2 * 2 * heads * (2 * part) ** 2 * (width + HEAD),
            bytes_accessed=rows * width * 30,
            transcendentals=2 * 2 * heads * (2 * part) ** 2,
        ),
        compiler_params=pltpu.CompilerParams(vmem_limit_bytes=24 * MIB),
        name="attend",
    )(
        qkv.reshape(2, 2, part, 3 * width),
        cosine.reshape(2, 2, part, table),
        sine.reshape(2, 2, part, table),
        mask,
    )
    return rot, out.reshape(rows, width), lse


def attend_back(rot, grad, lse, cosine, sine, mask):
    rows, width = grad.shape
    part, heads, table = rows // 4, width // HEAD, cosine.shape[1]
    out = pl.pallas_call(
        attend_back_kernel,
        grid=(2,),
        in_specs=[
            by_block(3 * width, part),
            by_block(width, part),
            pl.BlockSpec((1, heads, 2 * part), lambda i: (i, 0, 0)),
            by_block(table, part),
            by_block(table, part),
            pl.BlockSpec((1, 2 * part, 2 * part), lambda i: (i, 0, 0)),
        ],
        out_specs=by_block(3 * width, part),
        out_shape=jax.ShapeDtypeStruct((2, 2, part, 3 * width), bf16),
        scratch_shapes=[
            pltpu.VMEM((2 * part, width), f32),
            pltpu.VMEM((2 * part, width), f32),
            pltpu.VMEM((width, 2 * part), f32),
        ],
        cost_estimate=pl.CostEstimate(
            flops=2 * 2 * heads * (2 * part) ** 2 * (4 * width + HEAD),
            bytes_accessed=rows * width * 30,
            transcendentals=2 * heads * (2 * part) ** 2,
        ),
        compiler_params=pltpu.CompilerParams(vmem_limit_bytes=24 * MIB),
        name="attend_back",
    )(
        rot,
        grad.reshape(2, 2, part, width),
        lse,
        cosine.reshape(2, 2, part, table),
        sine.reshape(2, 2, part, table),
        mask,
    )
    return out.reshape(rows, 3 * width)


def local_dot(left, right):
    return jnp.dot(left, right, preferred_element_type=f32)


def dot_right_t(left, right):
    return lax.dot_general(left, right, (((1,), (1,)), ((), ())), preferred_element_type=f32)


def dot_left_t(left, right):
    return lax.dot_general(left, right, (((0,), (0,)), ((), ())), preferred_element_type=f32)


def transpose_kernel(value_ref, out_ref):
    out_ref[...] = value_ref[...].T


def transposed(value):
    rows, width = value.shape
    tile = width // 4
    return pl.pallas_call(
        transpose_kernel,
        grid=(4,),
        in_specs=[pl.BlockSpec((rows, tile), lambda i: (0, i))],
        out_specs=pl.BlockSpec((tile, rows), lambda i: (i, 0)),
        out_shape=jax.ShapeDtypeStruct((width, rows), value.dtype),
        cost_estimate=pl.CostEstimate(
            flops=0, bytes_accessed=4 * rows * width, transcendentals=0
        ),
        compiler_params=pltpu.CompilerParams(vmem_limit_bytes=8 * MIB),
        name="transposed",
    )(value)


def weight_grads_kernel(steps, left_ref, right_ref, *refs):
    out = refs[-1]
    columns = right_ref[...]
    tall = out.shape[0] // steps
    for start in range(0, out.shape[0], tall):
        out[start : start + tall, :] = local_dot(
            left_ref[start : start + tall, :], columns
        ).astype(bf16)


def weight_grads(left, right, tile, steps, columns, first, into=()):
    width, tokens = left.shape
    count = right.shape[1]
    anywhere = pl.BlockSpec(memory_space=pl.ANY)
    to = first // tile
    return pl.pallas_call(
        functools.partial(weight_grads_kernel, steps),
        grid=(count // tile,),
        in_specs=[
            pl.BlockSpec(memory_space=pltpu.VMEM),
            pl.BlockSpec((tokens, tile), lambda i: (0, i)),
        ]
        + [anywhere] * len(into),
        out_specs=pl.BlockSpec((width, tile), lambda i: (0, to + i)),
        out_shape=jax.ShapeDtypeStruct((width, columns), bf16),
        input_output_aliases={2 + k: k for k in range(len(into))},
        cost_estimate=pl.CostEstimate(
            flops=2 * tokens * width * count,
            bytes_accessed=2 * (tokens * width + (tokens + width) * count),
            transcendentals=0,
        ),
        compiler_params=pltpu.CompilerParams(vmem_limit_bytes=44 * MIB),
        name="weight_grads",
    )(left, right, *into)


def feed_kernel(normed_ref, cot_ref, gate_up_ref, down_ref, mixed_ref, grad_ref):
    units = mixed_ref.shape[1]
    gate_up = local_dot(normed_ref[...], gate_up_ref[...])
    gate, up = gate_up[:, :units], gate_up[:, units:]
    back = local_dot(cot_ref[...], down_ref[...])
    sigmoid = jax.nn.sigmoid(gate)
    silu = gate * sigmoid
    mixed_ref[...] = (silu * up).astype(bf16)
    grad_ref[:, :units] = (back * up * sigmoid * (1.0 + gate * (1.0 - sigmoid))).astype(bf16)
    grad_ref[:, units:] = (back * silu).astype(bf16)


def feed(normed, cot, full, units, tile):
    rows, width = normed.shape
    steps = units // tile
    return pl.pallas_call(
        feed_kernel,
        grid=(steps,),
        in_specs=[
            pl.BlockSpec((rows, width), lambda i: (0, 0)),
            pl.BlockSpec((rows, width), lambda i: (0, 0)),
            pl.BlockSpec((width, 2 * tile), lambda i: (0, i)),
            pl.BlockSpec((width, tile), lambda i: (0, 2 * steps + i)),
        ],
        out_specs=[
            pl.BlockSpec((rows, tile), lambda i: (0, i)),
            pl.BlockSpec((rows, 2 * tile), lambda i: (0, i)),
        ],
        out_shape=[
            jax.ShapeDtypeStruct((rows, units), bf16),
            jax.ShapeDtypeStruct((rows, 2 * units), bf16),
        ],
        cost_estimate=pl.CostEstimate(
            flops=6 * rows * width * units,
            bytes_accessed=2 * (2 * rows * width + 3 * (rows + width) * units),
            transcendentals=rows * units,
        ),
        compiler_params=pltpu.CompilerParams(vmem_limit_bytes=52 * MIB),
        name="feed",
    )(normed, cot, full, full)


def to_width_kernel(left_ref, full_ref, *refs):
    low_ref, high_ref = refs[-2:]
    rows = low_ref.shape[0]
    high_ref[...] = dot_right_t(left_ref[rows:, :], full_ref[...]).astype(bf16)
    low_ref[...] = dot_right_t(left_ref[:rows, :], full_ref[...]).astype(bf16)


def to_width(left, full, at, columns, first, into=()):
    rows, depth, width = left.shape[0] // 2, left.shape[1], full.shape[0]
    tile = width // 4
    to = first // tile
    anywhere = pl.BlockSpec(memory_space=pl.ANY)
    return pl.pallas_call(
        to_width_kernel,
        grid=(4,),
        in_specs=[
            pl.BlockSpec(memory_space=pltpu.VMEM),
            pl.BlockSpec((tile, depth), lambda i: (i, at)),
        ]
        + [anywhere] * len(into),
        out_specs=[pl.BlockSpec((rows, tile), lambda i: (0, to + i))] * 2,
        out_shape=[jax.ShapeDtypeStruct((rows, columns), bf16)] * 2,
        input_output_aliases={2 + k: k for k in range(len(into))},
        cost_estimate=pl.CostEstimate(
            flops=4 * rows * depth * width,
            bytes_accessed=2 * (2 * rows * depth + width * (2 * rows + depth)),
            transcendentals=0,
        ),
        compiler_params=pltpu.CompilerParams(vmem_limit_bytes=44 * MIB),
        name="to_width",
    )(left, full, *into)


INWARD = [(g // 8 * 2 + g % 2) * 4 + g // 2 % 4 for g in range(32)]
OUTWARD = [(n // 8 * 4 + n % 4) * 2 + n // 4 % 2 for n in range(32)]
BOTH_OUTWARD = OUTWARD + [32 + g for g in OUTWARD]


def middle_kernel(hidden_ref, own_ref, near_ref, far_ref, gain_ref, middle_ref, normed_ref):
    middle = hidden_ref[...].astype(f32) + own_ref[...].astype(f32)
    middle = middle + near_ref[...].astype(f32) + far_ref[...].astype(f32)
    scale = lax.rsqrt(jnp.mean(middle * middle, axis=-1, keepdims=True) + norm_epsilon)
    middle_ref[...] = middle
    normed_ref[...] = (middle * scale * gain_ref[...]).astype(bf16)


def middle_norm(hidden, terms, gain):
    whole = pl.BlockSpec(memory_space=pltpu.VMEM)
    return pl.pallas_call(
        middle_kernel,
        out_shape=[
            jax.ShapeDtypeStruct(hidden.shape, f32),
            jax.ShapeDtypeStruct(hidden.shape, bf16),
        ],
        in_specs=[whole] * 5,
        out_specs=[whole] * 2,
        compiler_params=pltpu.CompilerParams(vmem_limit_bytes=12 * MIB),
        name="middle_norm",
    )(hidden, *terms, gain)


def turn_kernel(groups, value_ref, out_ref):
    value = value_ref[...].astype(f32)
    chunk = value.shape[1] // len(groups)
    parts = [value[:, g * chunk : (g + 1) * chunk] for g in groups]
    out_ref[...] = jnp.concatenate(parts, axis=1).astype(bf16)


def turned(value, groups):
    whole = pl.BlockSpec(memory_space=pltpu.VMEM)
    return pl.pallas_call(
        functools.partial(turn_kernel, tuple(groups)),
        out_shape=jax.ShapeDtypeStruct(value.shape, bf16),
        in_specs=[whole],
        out_specs=whole,
        compiler_params=pltpu.CompilerParams(vmem_limit_bytes=16 * MIB),
        name="turned",
    )(value)


def inward(gain):
    return jnp.swapaxes(gain.reshape(4, 2, 4, -1), 1, 2).reshape(1, -1)


def outward(gains):
    return jnp.swapaxes(gains.reshape(2, 4, 4, 2, -1), 2, 3).reshape(2, -1)


def per_device(
    tokens,
    seq_lengths,
    attention_gain,
    feedforward_gain,
    query_weight,
    key_weight,
    value_weight,
    output_weight,
    gate_weight,
    up_weight,
    down_weight,
    cotangent,
):
    y, xh, z, xl, c = (lax.axis_index(a) for a in AXES)
    block, width = tokens.shape
    rows = block // 4
    chunk = width // 32
    pair, cross = x_ring[:2]
    stage = lax.optimization_barrier

    third = query_weight.shape[1] // 2
    units = gate_weight.shape[1] // 2
    tile = units // 4
    gain_one, gain_two = inward(attention_gain), inward(feedforward_gain)

    attention_tiles = [(k, 0, third) for k in range(4)]
    feed_tiles = [(k, j * tile, tile) for j in range(4) for k in range(2)] + [(2, 0, units)]
    sent = own_columns(
        (query_weight, key_weight, value_weight, output_weight.T),
        attention_tiles,
    )
    feed_blocks = (gate_weight, up_weight, down_weight.T)
    sent, feed_blocks, tokens, cotangent = stage((sent, feed_blocks, tokens, cotangent))
    attention_full = gather_weights(sent, xh)
    feed_full = gather_weights(own_columns(feed_blocks, feed_tiles), xh)
    offsets = line_offsets(rows, xl, c)
    tokens_in, cotangent_in = turned(tokens, INWARD), turned(cotangent, INWARD)
    other = cross(for_the_line(tokens_in, rows, offsets))
    sent = for_the_line(cotangent_in, rows, offsets)
    other, sent = stage((other, sent))
    cot_other = cross(sent)
    hidden_low = of_the_line(tokens_in, other, rows, offsets)
    x_own = hidden_low[:rows]

    lengths = jnp.stack([seq_lengths, cross(seq_lengths)])
    step = jnp.arange(block, dtype=jnp.int32)
    at_c, at_xl, at_row = step // (2 * rows), (step // rows) % 2, step % rows
    block_rows = ((xl ^ at_xl) * 2 + (c ^ at_c)) * rows + at_row
    segment, position = jax.vmap(layout, (0, None))(lengths, block_rows)
    mask = (segment[:, :, None] == segment[:, None, :]) & (
        block_rows[:, None] <= block_rows[None, :]
    )
    mask = mask.astype(f32)
    by_row = jnp.swapaxes(position.reshape(2, 2, block // 2), 0, 1).reshape(2 * block)
    cosine, sine = rotary(by_row)

    hidden = hidden_low.astype(f32)
    scale_one = lax.rsqrt(jnp.mean(hidden * hidden, axis=-1, keepdims=True) + norm_epsilon)
    normed_one = (hidden * scale_one * gain_one).astype(bf16)
    normed_one, mask, cosine, sine, cot_other = stage((normed_one, mask, cosine, sine, cot_other))
    cot = of_the_line(cotangent_in, cot_other, rows, offsets)
    c_own = cot[:rows]
    qkv_full, out_full = pack(
        [attention_full],
        [(0, 0, width, 0, 0, 0, 3 * third), (0, 0, width, 1, 0, 3 * third, third)],
        jnp.zeros((1,), jnp.int32),
        [(width, 3 * third), (width, third)],
    )
    qkv = local_dot(normed_one, qkv_full)
    rot, attended, lse = attend(qkv, cosine, sine, mask)
    from_core = core(dot_right_t(attended[block:], out_full).astype(bf16))
    parts = sum_split(
        [dot_right_t(attended[:block], out_full).astype(bf16), from_core], ring_cuts(block)
    )
    sides = ring_between(parts, ring_first(parts, x_ring))
    middle, n2_own = middle_norm(x_own, (parts[0], *both_ways(sides, x_ring)), gain_two)
    n2_sides = both_ways((n2_own, n2_own), x_ring)
    n1_turned, cot_turned = transposed(normed_one), transposed(cot)
    n2_sides, n1_turned, cot_turned = stage((n2_sides, n1_turned, cot_turned))
    n2_mine = stacked(ring_pieces(n2_own, n2_sides, opposite_halves(n2_sides, x_ring)))
    normed_two = stacked([n2_mine, core(n2_mine)])
    normed_two, n2_turned = stage((normed_two, transposed(normed_two)))

    mixed_low, gate_up_grad = feed(normed_two, cot, feed_full, units, tile)
    wide = units // 2
    gate_up_term = weight_grads(n2_turned, gate_up_grad, units // 2, 4, 2 * units, 0)
    gate_up_grad, gate_up_term, mixed_low = stage((gate_up_grad, gate_up_term, mixed_low))
    gate_up_sum = lax.psum_scatter(gate_up_term, ("y", "z"), scatter_dimension=0, tiled=True)
    mine, high = to_width(gate_up_grad, feed_full, 0, width, 0)
    mine, high, mixed_low = stage((mine, high, mixed_low))
    from_core = core(high)
    rest_term = weight_grads(cot_turned, mixed_low, units // 2, 4, units + 4 * third, 0)
    from_core, rest_term = stage((from_core, rest_term))
    parts = sum_split([mine, from_core], ring_cuts(block))
    arrived, mixed_low = stage((ring_first(parts, x_ring), mixed_low))
    sides = both_ways(ring_between(parts, arrived), x_ring)
    both = to_width(mixed_low, feed_full, 2, 2 * width, 0)
    sides, both = stage((sides, both))
    normed_two_grad = total([parts[0], *sides])
    scale_two = lax.rsqrt(jnp.mean(middle * middle, axis=-1, keepdims=True) + norm_epsilon)
    middle_unit = middle * scale_two
    weighted_two = normed_two_grad * gain_two
    middle_grad = c_own.astype(f32) + scale_two * (
        weighted_two - middle_unit * jnp.mean(weighted_two * middle_unit, axis=-1, keepdims=True)
    )
    gain_two_part = jnp.sum(normed_two_grad * middle_unit, axis=0, keepdims=True)
    middle_grad_low = line_gather(middle_grad.astype(bf16))

    attended_grad = local_dot(middle_grad_low, out_full).astype(bf16)
    qkv_grad = attend_back(rot, attended_grad, lse, cosine, sine, mask)
    rest_term = weight_grads(
        transposed(middle_grad_low),
        attended,
        third,
        4,
        units + 4 * third,
        units + 3 * third,
        (rest_term,),
    )
    rest_term = weight_grads(
        n1_turned, qkv_grad, third, 4, units + 4 * third, units, (rest_term,)
    )
    qkv_grad, rest_term = stage((qkv_grad, rest_term))
    rest_term, gate_up_sum = stage((rest_term, gate_up_sum))
    rest_sum = lax.psum_scatter(rest_term, ("y", "z"), scatter_dimension=0, tiled=True)

    mine, high = to_width(qkv_grad, qkv_full, 0, 2 * width, width, tuple(both))
    from_core = core(high)
    gain_one_part = jnp.sum(
        jnp.concatenate([mine[:, width:], high[:, width:]], axis=0).astype(f32)
        * (hidden * scale_one),
        axis=0,
        keepdims=True,
    )
    gains = jnp.concatenate([gain_one_part, gain_two_part], axis=0)
    gains_core = core(gains)
    parts = sum_split([mine, from_core], ring_cuts(block))
    arrived = ring_first(parts, x_ring)
    arrived, gains_core = stage((arrived, gains_core))

    sides = both_ways(ring_between(parts, arrived), x_ring)
    gains = gains + gains_core
    gains_ways = direct(gains, x_ring)
    (middle_back,) = by_tensor(
        [middle_grad_low], [(0, k * rows, k % 2, k // 4) for k in (0, 1, 4, 5)], rows, xl, c
    )
    middle_back = turned(middle_back, OUTWARD)
    sides, gains_ways, middle_back = stage((sides, gains_ways, middle_back))

    sums = total([parts[0], *sides])
    both_own = jnp.concatenate([middle + sums[:, :width], sums[:, width:]], axis=1)
    both_own = turned(both_own.astype(bf16), BOTH_OUTWARD)
    both_pair = pair(both_own)
    gains = sum_round(gains, gains_ways)
    gains_ways = direct(gains, y_ring)
    both_pair, gains_ways = stage((both_pair, gains_ways))

    both_core = core(stacked([both_own, both_pair]))
    gains = sum_round(gains, gains_ways)
    gains_ways = direct(gains, z_ring)
    feed_own = both_ways(to_columns(gate_up_sum[:chunk], gate_up_sum[chunk:], xh), x_ring)
    gains_ways, both_core, feed_own = stage((gains_ways, both_core, feed_own))

    gains = outward(sum_round(gains, gains_ways))
    layer_out, normed_one_grad = by_tensor(
        [both_own, both_pair, both_core],
        [(0, 0, 0, 0), (1, 0, 1, 0), (2, 0, 0, 1), (2, rows, 1, 1)],
        rows,
        xl,
        c,
        2,
    )
    normed_one_grad = normed_one_grad.astype(f32)
    gate_grad, up_grad = delivered(*feed_own, xh, feed_tiles[:-1], (2 * units,) * 2)
    own = tokens.astype(f32)
    own_scale = lax.rsqrt(jnp.mean(own * own, axis=-1, keepdims=True) + norm_epsilon)
    own_unit = own * own_scale
    weighted_one = normed_one_grad * attention_gain
    tokens_grad = middle_back.astype(f32) + own_scale * (
        weighted_one - own_unit * jnp.mean(weighted_one * own_unit, axis=-1, keepdims=True)
    )
    (tokens_grad, gains, gate_grad, up_grad, rest_sum) = stage(
        (tokens_grad, gains, gate_grad, up_grad, rest_sum)
    )
    rest_own = both_ways(to_columns(rest_sum[:chunk], rest_sum[chunk:], xh), x_ring)
    down_grad, query_grad, key_grad, value_grad, output_grad = delivered(
        *rest_own,
        xh,
        [(0, 0, units)] + [(k + 1, 0, third) for k in range(4)],
        (2 * units,) + (2 * third,) * 4,
    )
    return (
        layer_out,
        tokens_grad,
        gains[0],
        gains[1],
        query_grad,
        key_grad,
        value_grad,
        output_grad.T,
        gate_grad,
        up_grad,
        down_grad.T,
    )


def solution(mesh):
    named = Mesh(mesh.devices.reshape(SIZES), AXES)
    return jax.shard_map(
        per_device,
        mesh=named,
        in_specs=(
            P(DP, None),
            P(DP),
            P(),
            P(),
            P(DP, TP),
            P(DP, TP),
            P(DP, TP),
            P(TP, DP),
            P(DP, TP),
            P(DP, TP),
            P(TP, DP),
            P(DP, None),
        ),
        out_specs=(
            P(DP, None),
            P(DP, None),
            P(),
            P(),
            P(DP, TP),
            P(DP, TP),
            P(DP, TP),
            P(TP, DP),
            P(DP, TP),
            P(DP, TP),
            P(TP, DP),
        ),
        check_vma=False,
    )
```
